32 devices in a mesh: wide: 8 (over z, y), narrow: 4 (over x, core).
Axes of the slice: x: 2, y: 2, z: 4, core: 2. Of those that a mesh axis runs over, the one named last changes fastest.
Arguments:
- a_blocks: bfloat16 [6144, 64, 512], P(('wide', 'narrow')), may hold values from -0.25 to 0.25
- a_columns: int32 [6144, 8], P(('wide', 'narrow')), may hold values from 0 to 6143, as said below
- p_blocks: bfloat16 [6144, 64, 192], P(('wide', 'narrow')), may hold values from -0.75 to 0.75
- p_pattern: int32 [6144, 3], P(('wide', 'narrow')), may hold values from 0 to 1, as said below
- aggregate: int32 [6144], P(('wide', 'narrow')), may hold values from 0 to 63, as said below
- owner_map: int32 [64], replicated, may hold values from 0 to 31, as said below
Outputs:
- owned_coarse: bfloat16 [256, 64, 192], P(('wide', 'narrow'))
The draws below stay inside these ranges and needn't reach their ends.
Inputs may be any that keep to these rules, and one draw needn't show every extreme that they name: `a_columns`: entry 0 of row i is i; every entry lies within 32 rows of i; entries 1 and 2 are i - 32 and i + 32, clipped to 0 to 6143. `aggregate`: Non-decreasing; the aligned block of rows g * 192 to (g + 1) * 192 - 1 holds exactly aggregates g * 2 to (g + 1) * 2 - 1, each a run of 48 rows or more. `p_pattern`: entry 1 is always 1; entry 0 can be 1 only on the first 8 rows of an aggregate other than aggregate 0, entry 2 only on the last 8 rows of an aggregate other than the last one. `owner_map`: with N devices, N / 8 devices own exactly 8 aggregates each, N - N / 2 devices own exactly 2 each, and the others none; which devices is drawn.
All inputs are finite; a program needn't handle non-finite values.
Results may differ from the reference program's by a relative error of at most 0.005.
Values may be sent and summed in bfloat16 or wider, within the bound.
A program may use at most 128 MiB of HBM per device.

```python
import math
import jax
import jax.numpy as jnp
from jax import lax

B = 64
KA = 8
HR = 32
SPR = 8
LW = 2
OWNMAX = 8
R = 192
AMIN = 48
NB = 6144
NAGG = 64
N_WIDE = 8
N_NARROW = 4


def aggregate_layout(key):
    device_total = NAGG // LW
    spare_rows = R - LW * AMIN
    weights = jax.random.randint(jax.random.fold_in(key, 11), (device_total, LW), 1, 9)
    weights = weights.at[0, 0].set(0)
    cumulative = jnp.cumsum(weights, axis=1)
    before = cumulative - weights
    weight_total = cumulative[:, -1:]
    starts = AMIN * jnp.arange(LW, dtype=jnp.int32)[None, :] + spare_rows * before // weight_total
    row_ids = jnp.arange(R, dtype=jnp.int32)
    local_agg = jnp.sum((row_ids[None, :, None] >= starts[:, None, :]).astype(jnp.int32), axis=2) - 1
    ends = jnp.concatenate([starts[:, 1:], jnp.full((device_total, 1), R, jnp.int32)], axis=1)
    start_of = jnp.take_along_axis(starts, local_agg, axis=1)
    end_of = jnp.take_along_axis(ends, local_agg, axis=1)
    global_agg = local_agg + LW * jnp.arange(device_total, dtype=jnp.int32)[:, None]
    coin_flips = jax.random.randint(jax.random.fold_in(key, 12), (device_total, R, 3), 0, 2)
    near_start = row_ids[None, :] - start_of < SPR
    near_end = end_of - 1 - row_ids[None, :] < SPR
    lower_link = coin_flips[:, :, 0] * (near_start & (global_agg > 0)).astype(jnp.int32)
    upper_link = coin_flips[:, :, 2] * (near_end & (global_agg < NAGG - 1)).astype(jnp.int32)
    middle_link = jnp.ones_like(lower_link)
    pattern = jnp.stack([lower_link, middle_link, upper_link], axis=-1).astype(jnp.int32)
    return (global_agg.reshape(-1).astype(jnp.int32), pattern.reshape(-1, 3))


def draw_aggregate(key, part):
    return aggregate_layout(key)[0]


def draw_p_pattern(key, part):
    return aggregate_layout(key)[1]


def draw_a_columns(key, part):
    offsets = jax.random.randint(jax.random.fold_in(key, 21), (NB, KA), -HR, HR + 1)
    offsets = offsets.at[:, 0].set(0).at[:, 1].set(-HR).at[:, 2].set(HR)
    columns = jnp.arange(NB, dtype=jnp.int32)[:, None] + offsets
    return jnp.clip(columns, 0, NB - 1).astype(jnp.int32)


def draw_owner_map(key, part):
    device_total = NAGG // LW
    order = jax.random.permutation(jax.random.fold_in(key, 31), device_total).astype(jnp.int32)
    busy_total = device_total // OWNMAX
    ticket = jnp.arange(NAGG, dtype=jnp.int32)
    heavy_pick = jnp.clip(ticket // OWNMAX, 0, device_total - 1)
    light_pick = jnp.clip(busy_total + (ticket - device_total) // LW, 0, device_total - 1)
    holder = jnp.where(ticket < device_total, order[heavy_pick], order[light_pick])
    shuffle = jax.random.permutation(jax.random.fold_in(key, 32), NAGG)
    return holder[shuffle].astype(jnp.int32)


def block_scale(key, dims, split, low, high):
    factor_of = 1.0
    for position, shards_of in split:
        steps = jax.random.uniform(jax.random.fold_in(jax.random.fold_in(key, 6), position), (shards_of,), jnp.float32, low / len(split), high / len(split))
        factor_of = factor_of * jnp.repeat(jnp.exp(steps), dims[position] // shards_of).reshape((-1,) + (1,) * (len(dims) - 1 - position))
    return factor_of


def scatter_about(own_key, shape, width, most, split=(), kind=jnp.bfloat16):
    level = block_scale(own_key, shape, split, -0.22, 0.18) if split else 1.0
    drawn = jax.random.normal(own_key, shape, jnp.float32) * width * level
    return jnp.minimum(jnp.maximum(drawn, -most), most).astype(kind)


def setup_inputs(seed: int = 0) -> dict:
    splits = jax.random.split(jax.random.key(seed), 7)
    return {
        "a_blocks": scatter_about(splits[0], (NB, B, KA * B), (KA * B) ** -0.5, 0.25, ((0, 32),)),
        "a_columns": draw_a_columns(jax.random.fold_in(splits[6], 71), 0),
        "p_blocks": scatter_about(splits[2], (NB, B, 3 * B), B ** -0.5, 0.75, ((0, 32),)),
        "p_pattern": draw_p_pattern(jax.random.fold_in(splits[6], 71), 0),
        "aggregate": draw_aggregate(jax.random.fold_in(splits[6], 71), 0),
        "owner_map": draw_owner_map(jax.random.fold_in(splits[6], 71), 0),
    }


def reference(a_blocks, a_columns, p_blocks, p_pattern, aggregate, owner_map):
    device_total = N_WIDE * N_NARROW
    fine_total = a_blocks.shape[0]
    row_block = math.gcd(fine_total, 64)
    block_count = fine_total // row_block
    term_ids = jnp.arange(3, dtype=jnp.int32)

    def fetch_prolong(row_list):
        blocks = jnp.take(p_blocks, row_list, axis=0).astype(jnp.float32)
        blocks = blocks.reshape(row_list.shape + (B, 3, B))
        present = jnp.take(p_pattern, row_list, axis=0).astype(jnp.float32)
        return blocks * present[..., None, :, None]

    def accumulate_block(accum, block_index):
        first_row = (block_index * row_block).astype(jnp.int32)
        row_ids = first_row + jnp.arange(row_block, dtype=jnp.int32)
        a_part = lax.dynamic_slice_in_dim(a_blocks, first_row, row_block, 0).astype(jnp.float32)
        a_part = a_part.reshape(row_block, B, KA, B)
        col_part = jnp.take(a_columns, row_ids, axis=0)
        own_agg = jnp.take(aggregate, row_ids)
        far_agg = jnp.take(aggregate, col_part)
        own_p = fetch_prolong(row_ids)
        far_p = fetch_prolong(col_part)
        terms = jnp.einsum("inkx,ikxty->inkty", a_part, far_p)
        band = far_agg[:, :, None] + term_ids[None, None, :] - own_agg[:, None, None]
        chooser = (band[:, :, :, None] == term_ids[None, None, None, :]).astype(jnp.float32)
        applied = jnp.einsum("inkty,ikte->iney", terms, chooser).astype(jnp.bfloat16)
        applied = lax.optimization_barrier(applied).astype(jnp.float32)
        coarse = jnp.einsum("ixty,ixez->iteyz", own_p, applied)
        coarse_row = own_agg[:, None] + term_ids[None, :] - 1
        offset = term_ids[None, :] - term_ids[:, None] + 1
        inside = (offset[None] >= 0) & (offset[None] <= 2) & (coarse_row[:, :, None] >= 0) & (coarse_row[:, :, None] < NAGG)
        segment = jnp.where(inside, coarse_row[:, :, None] * 3 + offset[None], NAGG * 3)
        accum = accum + jax.ops.segment_sum(coarse.reshape(row_block * 9, B, B), segment.reshape(row_block * 9), num_segments=NAGG * 3 + 1)
        return accum, None

    start_accum = jnp.zeros((NAGG * 3 + 1, B, B), jnp.float32)
    accum, _ = lax.scan(accumulate_block, start_accum, jnp.arange(block_count, dtype=jnp.int32))
    coarse_rows = accum[:NAGG * 3].reshape(NAGG, 3, B, B).transpose(0, 2, 1, 3).reshape(NAGG, B, 3 * B)
    coarse_rows = coarse_rows.astype(jnp.bfloat16)
    one_hot = (owner_map[:, None] == jnp.arange(device_total, dtype=jnp.int32)[None, :]).astype(jnp.int32)
    owned_rank = jnp.sum(jnp.cumsum(one_hot, axis=0) * one_hot, axis=1) - 1
    placing = owner_map * OWNMAX + owned_rank
    result = jnp.zeros((device_total * OWNMAX, B, 3 * B), jnp.bfloat16).at[placing].set(coarse_rows)
    return result
```

```python
import jax
import jax.numpy as jnp
from jax import lax
from jax.experimental import pallas as pl
from jax.experimental.pallas import tpu as pltpu
from jax.sharding import PartitionSpec as P

HR = 32
LW = 2
OWNMAX = 8
GROUP = 8
AXES = ("wide", "narrow")


def place_rim(rim, keep_low):
    swapped = jnp.concatenate([rim[:, 64:], rim[:, :64]], axis=1)
    lane = lax.broadcasted_iota(jnp.int32, swapped.shape, 1)
    zero = jnp.zeros_like(swapped)
    low = jnp.where(lane < 64, swapped, zero)
    high = jnp.where(lane < 64, zero, swapped)
    return (low, high) if keep_low else (high, low)


def kernel(a_hbm, cols, p_hbm, pattern, aggregate, lower, upper, g_ref,
           a_v, p_v, pooled, applied, a_sem, p_sem):
    rows, nodes = a_hbm.shape[0], a_hbm.shape[1]
    me = lax.axis_index(AXES)
    groups = rows // GROUP
    shift = groups // 6

    def p_copy(g):
        span = pl.ds(g * GROUP, GROUP)
        return pltpu.make_async_copy(p_hbm.at[span], p_v.at[span], p_sem.at[g])

    def a_copy(g):
        span = pl.ds(g * GROUP, GROUP)
        return pltpu.make_async_copy(a_hbm.at[span], a_v.at[span], a_sem.at[g])

    @pl.loop(0, groups)
    def _(g):
        p_copy(g).start()

    @pl.loop(0, groups)
    def _(g):
        a_copy(lax.rem(g + shift, groups)).start()

    @pl.loop(0, HR)
    def _(i):
        low, high = place_rim(lower[i], True)
        pooled[i, :, :128] = low
        pooled[i, :, 128:] = high
        low, high = place_rim(upper[i], False)
        pooled[rows + HR + i, :, :128] = low
        pooled[rows + HR + i, :, 128:] = high

    left = lax.broadcasted_iota(jnp.int32, (nodes, 128), 1) < 64

    @pl.loop(0, groups)
    def _(g):
        p_copy(g).wait()
        for j in range(GROUP):
            i = g * GROUP + j
            second = aggregate[i] - me * LW == 1
            has0 = pattern[i, 0] == 1
            has2 = pattern[i, 2] == 1
            x0 = p_v[i, :, :128]
            x2 = p_v[i, :, 128:]
            swapped = jnp.concatenate([x0[:, 64:], x0[:, :64]], axis=1)
            twice = jnp.concatenate([x2, x2], axis=1)
            bit = lambda flag: jnp.where(flag, 1.0, 0.0).astype(jnp.bfloat16)
            one = jnp.ones_like(x0)
            first_low = jnp.where(left, swapped, twice * bit(has2))
            second_low = x0 * jnp.where(left, one * bit(has0), one)
            pooled[HR + i, :, :128] = first_low * bit(~second) + second_low * bit(second)
            pooled[HR + i, :, 128:] = jnp.where(
                left, twice * bit(has2 & second), swapped * bit(has0 & ~second)
            )

    g_ref[...] = jnp.zeros_like(g_ref)
    base = HR - me * rows

    def transposed_product(span_rows, lanes):
        left_rows = pooled[span_rows, :, lanes].reshape(GROUP * nodes, 128)
        return lax.dot_general(
            left_rows, applied[...], (((0,), (0,)), ((), ())), preferred_element_type=jnp.float32
        )

    @pl.loop(0, groups)
    def _(step):
        g = lax.rem(step + shift, groups)
        a_copy(g).wait()
        for j in range(GROUP):
            i = g * GROUP + j
            total = None
            for h in range(2):
                stack = jnp.concatenate(
                    [pooled[cols[i, 4 * h + k] + base] for k in range(4)], axis=0
                )
                part = jnp.dot(
                    a_v[i, :, 256 * h : 256 * (h + 1)], stack, preferred_element_type=jnp.float32
                )
                total = part if total is None else total + part
            applied[j * nodes : (j + 1) * nodes, :] = total.astype(jnp.bfloat16)
        g_ref[:128, :] += transposed_product(pl.ds(HR + g * GROUP, GROUP), pl.ds(0, 128))

        @pl.when((g == 0) | (g == groups - 1))
        def _():
            g_ref[128:, :] += transposed_product(pl.ds(HR + g * GROUP, GROUP), pl.ds(128, 128))


def pack(row):
    row = row.astype(jnp.bfloat16)
    tail = jnp.concatenate([row[:32, 128:], row[32:, 128:]], axis=1)
    return jnp.concatenate([row[:, :128], tail], axis=0)


def select_kernel(owner_map, every, out):
    me = lax.axis_index(AXES)
    out[...] = jnp.zeros_like(out)

    def visit(a, slot):
        @pl.when((owner_map[a] == me) & (slot < OWNMAX))
        def _():
            out[slot, :, :128] = every[a, :64, :]
            out[slot, :32, 128:] = every[a, 64:, :64]
            out[slot, 32:, 128:] = every[a, 64:, 64:]

        return slot + jnp.where(owner_map[a] == me, 1, 0)

    lax.fori_loop(0, owner_map.shape[0], visit, jnp.int32(0))


def shards(a_blocks, a_columns, p_blocks, p_pattern, aggregate, owner_map):
    rows, nodes = a_blocks.shape[:2]
    count = lax.axis_size(AXES)
    me = lax.axis_index(AXES)
    up = [(i, i + 1) for i in range(count - 1)]
    down = [(i + 1, i) for i in range(count - 1)]
    lanes = jnp.arange(2 * nodes) < nodes
    tail_keep = lanes[None, None, :] | (p_pattern[rows - HR :, 2] == 1)[:, None, None]
    head_keep = ~lanes[None, None, :] | (p_pattern[:HR, 0] == 1)[:, None, None]
    zero = jnp.zeros((), jnp.bfloat16)
    tail = jnp.where(tail_keep, p_blocks[rows - HR :, :, nodes:], zero)
    head = jnp.where(head_keep, p_blocks[:HR, :, : 2 * nodes], zero)
    lower = lax.ppermute(tail, AXES, up)
    upper = lax.ppermute(head, AXES, down)
    vmem = pl.BlockSpec(memory_space=pltpu.VMEM)
    smem = pl.BlockSpec(memory_space=pltpu.SMEM)
    hbm = pl.BlockSpec(memory_space=pl.ANY)
    groups = rows // GROUP
    total = pl.pallas_call(
        kernel,
        out_shape=jax.ShapeDtypeStruct((4 * nodes, 4 * nodes), jnp.float32),
        in_specs=[hbm, smem, hbm, smem, smem, vmem, vmem],
        out_specs=vmem,
        scratch_shapes=[
            pltpu.VMEM(a_blocks.shape, jnp.bfloat16),
            pltpu.VMEM(p_blocks.shape, jnp.bfloat16),
            pltpu.VMEM((rows + 2 * HR, nodes, 4 * nodes), jnp.bfloat16),
            pltpu.VMEM((GROUP * nodes, 4 * nodes), jnp.bfloat16),
            pltpu.SemaphoreType.DMA((groups,)),
            pltpu.SemaphoreType.DMA((groups,)),
        ],
        compiler_params=pltpu.CompilerParams(vmem_limit_bytes=48 << 20),
    )(a_blocks, a_columns, p_blocks, p_pattern, aggregate, lower, upper)
    block = total.reshape(4, nodes, 4, nodes)
    from_prev = lax.ppermute(jnp.concatenate([block[2, :, 1], block[2, :, 2]], 1), AXES, up)
    from_next = lax.ppermute(jnp.concatenate([block[3, :, 3], block[3, :, 0]], 1), AXES, down)
    pad = jnp.zeros((nodes, nodes), jnp.float32)
    first = jnp.concatenate([block[0, :, 3], block[0, :, 0], block[0, :, 1]], 1)
    second = jnp.concatenate([block[1, :, 0], block[1, :, 1], block[1, :, 2]], 1)
    first = first + jnp.concatenate([from_prev, pad], 1)
    second = second + jnp.concatenate([pad, from_next], 1)
    mine = jnp.stack([pack(first), pack(second)])
    every = lax.all_gather(mine, AXES, axis=0, tiled=True)
    return pl.pallas_call(
        select_kernel,
        out_shape=jax.ShapeDtypeStruct((OWNMAX, nodes, 3 * nodes), jnp.bfloat16),
        in_specs=[smem, vmem],
        out_specs=vmem,
        compiler_params=pltpu.CompilerParams(vmem_limit_bytes=32 << 20),
    )(owner_map, every)


def solution(mesh):
    placed = (
        P(AXES, None, None),
        P(AXES, None),
        P(AXES, None, None),
        P(AXES, None),
        P(AXES),
        P(),
    )
    return jax.shard_map(
        shards,
        mesh=mesh,
        in_specs=placed,
        out_specs=P(AXES, None, None),
        check_vma=False,
    )
```

```python
import functools

import jax
import jax.numpy as jnp
from jax import lax
from jax.experimental import pallas as pl
from jax.experimental.pallas import tpu as pltpu
from jax.sharding import PartitionSpec as P

HR = 32
LW = 2
OWNMAX = 8
GROUP = 8
AXES = ("wide", "narrow")


def place_rim(rim, keep_low):
    swapped = jnp.concatenate([rim[:, 64:], rim[:, :64]], axis=1)
    lane = lax.broadcasted_iota(jnp.int32, swapped.shape, 1)
    zero = jnp.zeros_like(swapped)
    low = jnp.where(lane < 64, swapped, zero)
    high = jnp.where(lane < 64, zero, swapped)
    return (low, high) if keep_low else (high, low)


def kernel(a_hbm, cols, p_hbm, pattern, aggregate, lower, upper, g_ref,
           a_v, p_v, pooled, applied, a_sem, p_sem):
    rows, nodes = a_hbm.shape[0], a_hbm.shape[1]
    me = lax.axis_index(AXES)
    groups = rows // GROUP
    shift = groups // 6

    def p_copy(g):
        span = pl.ds(g * GROUP, GROUP)
        return pltpu.make_async_copy(p_hbm.at[span], p_v.at[span], p_sem.at[g])

    def a_copy(g):
        span = pl.ds(g * GROUP, GROUP)
        return pltpu.make_async_copy(a_hbm.at[span], a_v.at[span], a_sem.at[g])

    @pl.loop(0, groups)
    def _(g):
        p_copy(g).start()

    @pl.loop(0, groups)
    def _(g):
        a_copy(lax.rem(g + shift, groups)).start()

    @pl.loop(0, HR)
    def _(i):
        low, high = place_rim(lower[i], True)
        pooled[i, :, :128] = low
        pooled[i, :, 128:] = high
        low, high = place_rim(upper[i], False)
        pooled[rows + HR + i, :, :128] = low
        pooled[rows + HR + i, :, 128:] = high

    left = lax.broadcasted_iota(jnp.int32, (nodes, 128), 1) < 64

    @pl.loop(0, groups)
    def _(g):
        p_copy(g).wait()
        for j in range(GROUP):
            i = g * GROUP + j
            second = aggregate[i] - me * LW == 1
            has0 = pattern[i, 0] == 1
            has2 = pattern[i, 2] == 1
            x0 = p_v[i, :, :128]
            x2 = p_v[i, :, 128:]
            swapped = jnp.concatenate([x0[:, 64:], x0[:, :64]], axis=1)
            twice = jnp.concatenate([x2, x2], axis=1)
            bit = lambda flag: jnp.where(flag, 1.0, 0.0).astype(jnp.bfloat16)
            one = jnp.ones_like(x0)
            first_low = jnp.where(left, swapped, twice * bit(has2))
            second_low = x0 * jnp.where(left, one * bit(has0), one)
            pooled[HR + i, :, :128] = first_low * bit(~second) + second_low * bit(second)
            pooled[HR + i, :, 128:] = jnp.where(
                left, twice * bit(has2 & second), swapped * bit(has0 & ~second)
            )

    g_ref[...] = jnp.zeros_like(g_ref)
    base = HR - me * rows

    def transposed_product(span_rows, lanes):
        left_rows = pooled[span_rows, :, lanes].reshape(GROUP * nodes, 128)
        return lax.dot_general(
            left_rows, applied[...], (((0,), (0,)), ((), ())), preferred_element_type=jnp.float32
        )

    @pl.loop(0, groups)
    def _(step):
        g = lax.rem(step + shift, groups)
        a_copy(g).wait()
        for j in range(GROUP):
            i = g * GROUP + j
            total = None
            for h in range(2):
                stack = jnp.concatenate(
                    [pooled[cols[i, 4 * h + k] + base] for k in range(4)], axis=0
                )
                part = jnp.dot(
                    a_v[i, :, 256 * h : 256 * (h + 1)], stack, preferred_element_type=jnp.float32
                )
                total = part if total is None else total + part
            applied[j * nodes : (j + 1) * nodes, :] = total.astype(jnp.bfloat16)
        g_ref[:128, :] += transposed_product(pl.ds(HR + g * GROUP, GROUP), pl.ds(0, 128))

        @pl.when((g == 0) | (g == groups - 1))
        def _():
            g_ref[128:, :] += transposed_product(pl.ds(HR + g * GROUP, GROUP), pl.ds(128, 128))


def gather_kernel(wide, narrow, total, owner_map, out, edge_out, edge_in, every,
                  edge_send, edge_recv, send_sem, recv_sem):
    w, n = lax.axis_index("wide"), lax.axis_index("narrow")
    me = w * narrow + n
    nodes = out.shape[1]
    count = wide * narrow
    following, preceding = lax.rem(me + 1, count), lax.rem(me + count - 1, count)
    beside = n + 1 - 2 * lax.rem(n, 2)
    across = lax.rem(n + 2, 4)
    mesh_id = pl.DeviceIdType.MESH

    barrier = pltpu.get_barrier_semaphore()
    for other in (following, preceding):
        pl.semaphore_signal(
            barrier, inc=1, device_id=(other // narrow, lax.rem(other, narrow)), device_id_type=mesh_id
        )
    for other in (beside, across):
        pl.semaphore_signal(barrier, inc=1, device_id=(w, other), device_id_type=mesh_id)

    def greet(d, carry):
        pl.semaphore_signal(
            barrier, inc=1, device_id=(lax.rem(w + d, wide), n), device_id_type=mesh_id
        )
        return carry

    lax.fori_loop(1, wide, greet, 0)

    edge_out[0] = total[2 * nodes : 3 * nodes, nodes : 3 * nodes]
    edge_out[1] = jnp.concatenate(
        [total[3 * nodes :, 3 * nodes :], total[3 * nodes :, :nodes]], axis=1
    )
    pl.semaphore_wait(barrier, wide + 3)

    def edge_copy(side, other):
        return pltpu.make_async_remote_copy(
            src_ref=edge_out.at[side],
            dst_ref=edge_in.at[side],
            send_sem=edge_send.at[side],
            recv_sem=edge_recv.at[side],
            device_id=(other // narrow, lax.rem(other, narrow)),
            device_id_type=mesh_id,
        )

    edges = [edge_copy(0, following), edge_copy(1, preceding)]
    for edge in edges:
        edge.start()
    for edge in edges:
        edge.wait()

    def store(slot, which, front, tail):
        every[slot, which, :64, :] = front.astype(jnp.bfloat16)
        tail = tail.astype(jnp.bfloat16)
        every[slot, which, 64:, :] = jnp.concatenate([tail[:32], tail[32:]], axis=1)

    own = jnp.concatenate([total[:nodes, 3 * nodes :], total[:nodes, :nodes]], axis=1)
    store(me, 0, own + edge_in[0], total[:nodes, nodes : 2 * nodes])
    own = total[nodes : 2 * nodes, : 2 * nodes]
    extra = edge_in[1]
    moved = jnp.concatenate([jnp.zeros_like(extra[:, :nodes]), extra[:, :nodes]], axis=1)
    last = total[nodes : 2 * nodes, 2 * nodes : 3 * nodes] + extra[:, nodes:]
    store(me, 1, own + moved, last)

    def copy(kind, d, slot, device):
        return pltpu.make_async_remote_copy(
            src_ref=every.at[slot],
            dst_ref=every.at[slot],
            send_sem=send_sem.at[kind, d],
            recv_sem=recv_sem.at[slot],
            device_id=device,
            device_id_type=mesh_id,
        )

    def along(d):
        return copy(0, d, me, (lax.rem(w + d, wide), n))

    def forward(d):
        slot = lax.rem(w + wide - d, wide) * narrow + n
        return copy(1, d, slot, (w, across)), copy(2, d, slot, (w, beside))

    def relay(d):
        slot = lax.rem(w + wide - d, wide) * narrow + across
        return copy(3, d, slot, (w, beside))

    def slot_at(d, column):
        return lax.rem(w + wide - d, wide) * narrow + column

    def send_along(d, carry):
        along(d).start()
        return carry

    lax.fori_loop(1, wide, send_along, 0)

    def pass_on(d, carry):
        @pl.when(d > 0)
        def _():
            copy(0, d, slot_at(d, n), (w, across)).wait_recv()

        for c in forward(d):
            c.start()
        return carry

    lax.fori_loop(0, wide, pass_on, 0)

    def pass_second(d, carry):
        copy(1, d, slot_at(d, across), (w, across)).wait_recv()
        relay(d).start()
        return carry

    lax.fori_loop(0, wide, pass_second, 0)

    def visit(a, found):
        hit = owner_map[a] == me
        rank = found[0]
        spots = tuple(
            jnp.where(hit & (rank == s), a, spot) for s, spot in enumerate(found[1:])
        )
        return (rank + jnp.where(hit, 1, 0),) + spots

    found = lax.fori_loop(
        0, owner_map.shape[0], visit, (jnp.int32(0),) + (jnp.int32(0),) * OWNMAX
    )

    across_beside = lax.rem(beside + 2, 4)

    def finish(d, carry):
        copy(2, d, slot_at(d, beside), (w, beside)).wait_recv()
        copy(3, d, slot_at(d, across_beside), (w, beside)).wait_recv()
        for c in forward(d):
            c.wait_send()
        relay(d).wait_send()

        @pl.when(d > 0)
        def _():
            along(d).wait_send()

        return carry

    lax.fori_loop(0, wide, finish, 0)

    for s in range(OWNMAX):
        spot = found[1 + s]
        keep = jnp.where(s < found[0], 1.0, 0.0)
        row = every[spot // LW, lax.rem(spot, LW)].astype(jnp.float32) * keep
        row = row.astype(jnp.bfloat16)
        out[s, :, :128] = row[:64]
        out[s, :32, 128:] = row[64:, :64]
        out[s, 32:, 128:] = row[64:, 64:]


def shards(a_blocks, a_columns, p_blocks, p_pattern, aggregate, owner_map):
    rows, nodes = a_blocks.shape[:2]
    count = lax.axis_size(AXES)
    up = [(i, i + 1) for i in range(count - 1)]
    down = [(i + 1, i) for i in range(count - 1)]
    lanes = jnp.arange(2 * nodes) < nodes
    tail_keep = lanes[None, None, :] | (p_pattern[rows - HR :, 2] == 1)[:, None, None]
    head_keep = ~lanes[None, None, :] | (p_pattern[:HR, 0] == 1)[:, None, None]
    zero = jnp.zeros((), jnp.bfloat16)
    tail = jnp.where(tail_keep, p_blocks[rows - HR :, :, nodes:], zero)
    head = jnp.where(head_keep, p_blocks[:HR, :, : 2 * nodes], zero)
    lower = lax.ppermute(tail, AXES, up)
    upper = lax.ppermute(head, AXES, down)
    vmem = pl.BlockSpec(memory_space=pltpu.VMEM)
    smem = pl.BlockSpec(memory_space=pltpu.SMEM)
    hbm = pl.BlockSpec(memory_space=pl.ANY)
    groups = rows // GROUP
    total = pl.pallas_call(
        kernel,
        out_shape=jax.ShapeDtypeStruct((4 * nodes, 4 * nodes), jnp.float32),
        in_specs=[hbm, smem, hbm, smem, smem, vmem, vmem],
        out_specs=vmem,
        scratch_shapes=[
            pltpu.VMEM(a_blocks.shape, jnp.bfloat16),
            pltpu.VMEM(p_blocks.shape, jnp.bfloat16),
            pltpu.VMEM((rows + 2 * HR, nodes, 4 * nodes), jnp.bfloat16),
            pltpu.VMEM((GROUP * nodes, 4 * nodes), jnp.bfloat16),
            pltpu.SemaphoreType.DMA((groups,)),
            pltpu.SemaphoreType.DMA((groups,)),
        ],
        compiler_params=pltpu.CompilerParams(vmem_limit_bytes=48 << 20),
    )(a_blocks, a_columns, p_blocks, p_pattern, aggregate, lower, upper)
    wide, narrow = lax.axis_size("wide"), lax.axis_size("narrow")
    return pl.pallas_call(
        functools.partial(gather_kernel, wide, narrow),
        out_shape=jax.ShapeDtypeStruct((OWNMAX, nodes, 3 * nodes), jnp.bfloat16),
        in_specs=[vmem, smem],
        out_specs=vmem,
        scratch_shapes=[
            pltpu.VMEM((2, nodes, 2 * nodes), jnp.float32),
            pltpu.VMEM((2, nodes, 2 * nodes), jnp.float32),
            pltpu.VMEM((count, LW, 96, 128), jnp.bfloat16),
            pltpu.SemaphoreType.DMA((2,)),
            pltpu.SemaphoreType.DMA((2,)),
            pltpu.SemaphoreType.DMA((4, wide)),
            pltpu.SemaphoreType.DMA((count,)),
        ],
        compiler_params=pltpu.CompilerParams(
            collective_id=0, has_side_effects=True, vmem_limit_bytes=32 << 20
        ),
    )(total, owner_map)


def solution(mesh):
    placed = (
        P(AXES, None, None),
        P(AXES, None),
        P(AXES, None, None),
        P(AXES, None),
        P(AXES),
        P(),
    )
    return jax.shard_map(
        shards,
        mesh=mesh,
        in_specs=placed,
        out_specs=P(AXES, None, None),
        check_vma=False,
    )
```

```python
import functools

import jax
import jax.numpy as jnp
from jax import lax
from jax.experimental import pallas as pl
from jax.experimental.pallas import tpu as pltpu
from jax.sharding import PartitionSpec as P

HR = 32
LW = 2
OWNMAX = 8
GROUP = 8
AXES = ("wide", "narrow")


def kernel(a_hbm, cols, p_hbm, pattern, aggregate, g_ref,
           a_v, p_v, pooled, applied, rim, a_sem, p_sem, send_sem, recv_sem):
    rows, nodes = a_hbm.shape[0], a_hbm.shape[1]
    me = lax.axis_index(AXES)
    groups = rows // GROUP
    shift = HR // GROUP
    narrow = lax.axis_size("narrow")
    count = lax.axis_size(AXES)
    mesh_id = pl.DeviceIdType.MESH
    others = [lax.rem(me + 1, count), lax.rem(me + count - 1, count)]
    others = [(other // narrow, lax.rem(other, narrow)) for other in others]
    barrier = pltpu.get_barrier_semaphore()
    for other in others:
        pl.semaphore_signal(barrier, inc=1, device_id=other, device_id_type=mesh_id)

    def p_copy(g):
        span = pl.ds(g * GROUP, GROUP)
        return pltpu.make_async_copy(p_hbm.at[span], p_v.at[span], p_sem.at[g])

    def a_copy(g):
        span = pl.ds(g * GROUP, GROUP)
        return pltpu.make_async_copy(a_hbm.at[span], a_v.at[span], a_sem.at[g])

    @pl.loop(0, groups)
    def _(g):
        p_copy(g).start()

    @pl.loop(0, groups)
    def _(g):
        a_copy(lax.rem(g + shift, groups)).start()

    left = lax.broadcasted_iota(jnp.int32, (nodes, 128), 1) < 64

    @pl.loop(0, groups)
    def _(g):
        p_copy(g).wait()
        for j in range(GROUP):
            i = g * GROUP + j
            second = aggregate[i] - me * LW == 1
            has0 = pattern[i, 0] == 1
            has2 = pattern[i, 2] == 1
            x0 = p_v[i, :, :128]
            x2 = p_v[i, :, 128:]
            swapped = jnp.concatenate([x0[:, 64:], x0[:, :64]], axis=1)
            twice = jnp.concatenate([x2, x2], axis=1)
            bit = lambda flag: jnp.where(flag, 1.0, 0.0).astype(jnp.bfloat16)
            one = jnp.ones_like(x0)
            first_low = jnp.where(left, swapped, twice * bit(has2))
            second_low = x0 * jnp.where(left, one * bit(has0), one)
            pooled[HR + i, :, :128] = first_low * bit(~second) + second_low * bit(second)
            pooled[HR + i, :, 128:] = jnp.where(
                left, twice * bit(has2 & second), swapped * bit(has0 & ~second)
            )

    def rim_copy(side):
        first = rows if side == 0 else HR
        return pltpu.make_async_remote_copy(
            src_ref=pooled.at[pl.ds(first, HR)],
            dst_ref=rim.at[side],
            send_sem=send_sem.at[side],
            recv_sem=recv_sem.at[side],
            device_id=others[side],
            device_id_type=mesh_id,
        )

    pl.semaphore_wait(barrier, 2)
    for side in range(2):
        rim_copy(side).start()

    g_ref[...] = jnp.zeros_like(g_ref)
    base = HR - me * rows
    limit = pooled.shape[0] - 1

    def transposed_product(span_rows, lanes):
        left_rows = pooled[span_rows, :, lanes].reshape(GROUP * nodes, 128)
        return lax.dot_general(
            left_rows, applied[...], (((0,), (0,)), ((), ())), preferred_element_type=jnp.float32
        )

    def run_group(step):
        g = lax.rem(step + shift, groups)
        a_copy(g).wait()
        for j in range(GROUP):
            i = g * GROUP + j
            total = None
            for h in range(2):
                stack = jnp.concatenate(
                    [pooled[jnp.clip(cols[i, 4 * h + k] + base, 0, limit)] for k in range(4)], axis=0
                )
                part = jnp.dot(
                    a_v[i, :, 256 * h : 256 * (h + 1)], stack, preferred_element_type=jnp.float32
                )
                total = part if total is None else total + part
            applied[j * nodes : (j + 1) * nodes, :] = total.astype(jnp.bfloat16)
        g_ref[:128, :] += transposed_product(pl.ds(HR + g * GROUP, GROUP), pl.ds(0, 128))

        @pl.when((g == 0) | (g == groups - 1))
        def _():
            g_ref[128:, :] += transposed_product(pl.ds(HR + g * GROUP, GROUP), pl.ds(128, 128))

    inner = groups - 2 * shift
    pl.loop(0, inner)(run_group)
    for side in range(2):
        rim_copy(side).wait()

    @pl.loop(0, HR)
    def _(i):
        for side, first in enumerate((0, rows + HR)):
            pooled[first + i, :, :128] = rim[side, i, :, 128:]
            pooled[first + i, :, 128:] = rim[side, i, :, :128]

    pl.loop(inner, groups)(run_group)


def gather_kernel(wide, narrow, total, owner_map, out, edge_out, edge_in, every,
                  edge_send, edge_recv, send_sem, recv_sem):
    w, n = lax.axis_index("wide"), lax.axis_index("narrow")
    me = w * narrow + n
    nodes = out.shape[1]
    count = wide * narrow
    following, preceding = lax.rem(me + 1, count), lax.rem(me + count - 1, count)
    beside = n + 1 - 2 * lax.rem(n, 2)
    across = lax.rem(n + 2, 4)
    mesh_id = pl.DeviceIdType.MESH

    barrier = pltpu.get_barrier_semaphore()
    for other in (following, preceding):
        pl.semaphore_signal(
            barrier, inc=1, device_id=(other // narrow, lax.rem(other, narrow)), device_id_type=mesh_id
        )
    for other in (beside, across):
        pl.semaphore_signal(barrier, inc=1, device_id=(w, other), device_id_type=mesh_id)

    def greet(d, carry):
        pl.semaphore_signal(
            barrier, inc=1, device_id=(lax.rem(w + d, wide), n), device_id_type=mesh_id
        )
        return carry

    lax.fori_loop(1, wide, greet, 0)

    edge_out[0] = total[2 * nodes : 3 * nodes, nodes : 3 * nodes]
    edge_out[1] = jnp.concatenate(
        [total[3 * nodes :, 3 * nodes :], total[3 * nodes :, :nodes]], axis=1
    )
    pl.semaphore_wait(barrier, wide + 3)

    def edge_copy(side, other):
        return pltpu.make_async_remote_copy(
            src_ref=edge_out.at[side],
            dst_ref=edge_in.at[side],
            send_sem=edge_send.at[side],
            recv_sem=edge_recv.at[side],
            device_id=(other // narrow, lax.rem(other, narrow)),
            device_id_type=mesh_id,
        )

    edges = [edge_copy(0, following), edge_copy(1, preceding)]
    for edge in edges:
        edge.start()
    for edge in edges:
        edge.wait()

    def store(slot, which, front, tail):
        every[slot, which, :64, :] = front.astype(jnp.bfloat16)
        tail = tail.astype(jnp.bfloat16)
        every[slot, which, 64:, :] = jnp.concatenate([tail[:32], tail[32:]], axis=1)

    own = jnp.concatenate([total[:nodes, 3 * nodes :], total[:nodes, :nodes]], axis=1)
    store(me, 0, own + edge_in[0], total[:nodes, nodes : 2 * nodes])
    own = total[nodes : 2 * nodes, : 2 * nodes]
    extra = edge_in[1]
    moved = jnp.concatenate([jnp.zeros_like(extra[:, :nodes]), extra[:, :nodes]], axis=1)
    last = total[nodes : 2 * nodes, 2 * nodes : 3 * nodes] + extra[:, nodes:]
    store(me, 1, own + moved, last)

    def copy(kind, d, slot, device):
        return pltpu.make_async_remote_copy(
            src_ref=every.at[slot],
            dst_ref=every.at[slot],
            send_sem=send_sem.at[kind, d],
            recv_sem=recv_sem.at[slot],
            device_id=device,
            device_id_type=mesh_id,
        )

    def along(d):
        return copy(0, d, me, (lax.rem(w + d, wide), n))

    def forward(d):
        slot = lax.rem(w + wide - d, wide) * narrow + n
        return copy(1, d, slot, (w, across)), copy(2, d, slot, (w, beside))

    def relay(d):
        slot = lax.rem(w + wide - d, wide) * narrow + across
        return copy(3, d, slot, (w, beside))

    def slot_at(d, column):
        return lax.rem(w + wide - d, wide) * narrow + column

    def send_along(d, carry):
        along(d).start()
        return carry

    lax.fori_loop(1, wide, send_along, 0)

    def pass_on(d, carry):
        @pl.when(d > 0)
        def _():
            copy(0, d, slot_at(d, n), (w, across)).wait_recv()

        for c in forward(d):
            c.start()
        return carry

    lax.fori_loop(0, wide, pass_on, 0)

    def pass_second(d, carry):
        copy(1, d, slot_at(d, across), (w, across)).wait_recv()
        relay(d).start()
        return carry

    lax.fori_loop(0, wide, pass_second, 0)

    def visit(a, found):
        hit = owner_map[a] == me
        rank = found[0]
        spots = tuple(
            jnp.where(hit & (rank == s), a, spot) for s, spot in enumerate(found[1:])
        )
        return (rank + jnp.where(hit, 1, 0),) + spots

    found = lax.fori_loop(
        0, owner_map.shape[0], visit, (jnp.int32(0),) + (jnp.int32(0),) * OWNMAX
    )

    across_beside = lax.rem(beside + 2, 4)

    def finish(d, carry):
        copy(2, d, slot_at(d, beside), (w, beside)).wait_recv()
        copy(3, d, slot_at(d, across_beside), (w, beside)).wait_recv()
        for c in forward(d):
            c.wait_send()
        relay(d).wait_send()

        @pl.when(d > 0)
        def _():
            along(d).wait_send()

        return carry

    lax.fori_loop(0, wide, finish, 0)

    for s in range(OWNMAX):
        spot = found[1 + s]
        keep = jnp.where(s < found[0], 1.0, 0.0)
        row = every[spot // LW, lax.rem(spot, LW)].astype(jnp.float32) * keep
        row = row.astype(jnp.bfloat16)
        out[s, :, :128] = row[:64]
        out[s, :32, 128:] = row[64:, :64]
        out[s, 32:, 128:] = row[64:, 64:]


def shards(a_blocks, a_columns, p_blocks, p_pattern, aggregate, owner_map):
    rows, nodes = a_blocks.shape[:2]
    count = lax.axis_size(AXES)
    vmem = pl.BlockSpec(memory_space=pltpu.VMEM)
    smem = pl.BlockSpec(memory_space=pltpu.SMEM)
    hbm = pl.BlockSpec(memory_space=pl.ANY)
    groups = rows // GROUP
    total = pl.pallas_call(
        kernel,
        out_shape=jax.ShapeDtypeStruct((4 * nodes, 4 * nodes), jnp.float32),
        in_specs=[hbm, smem, hbm, smem, smem],
        out_specs=vmem,
        scratch_shapes=[
            pltpu.VMEM(a_blocks.shape, jnp.bfloat16),
            pltpu.VMEM(p_blocks.shape, jnp.bfloat16),
            pltpu.VMEM((rows + 2 * HR, nodes, 4 * nodes), jnp.bfloat16),
            pltpu.VMEM((GROUP * nodes, 4 * nodes), jnp.bfloat16),
            pltpu.VMEM((2, HR, nodes, 4 * nodes), jnp.bfloat16),
            pltpu.SemaphoreType.DMA((groups,)),
            pltpu.SemaphoreType.DMA((groups,)),
            pltpu.SemaphoreType.DMA((2,)),
            pltpu.SemaphoreType.DMA((2,)),
        ],
        compiler_params=pltpu.CompilerParams(
            collective_id=1, has_side_effects=True, vmem_limit_bytes=48 << 20
        ),
    )(a_blocks, a_columns, p_blocks, p_pattern, aggregate)
    wide, narrow = lax.axis_size("wide"), lax.axis_size("narrow")
    return pl.pallas_call(
        functools.partial(gather_kernel, wide, narrow),
        out_shape=jax.ShapeDtypeStruct((OWNMAX, nodes, 3 * nodes), jnp.bfloat16),
        in_specs=[vmem, smem],
        out_specs=vmem,
        scratch_shapes=[
            pltpu.VMEM((2, nodes, 2 * nodes), jnp.float32),
            pltpu.VMEM((2, nodes, 2 * nodes), jnp.float32),
            pltpu.VMEM((count, LW, 96, 128), jnp.bfloat16),
            pltpu.SemaphoreType.DMA((2,)),
            pltpu.SemaphoreType.DMA((2,)),
            pltpu.SemaphoreType.DMA((4, wide)),
            pltpu.SemaphoreType.DMA((count,)),
        ],
        compiler_params=pltpu.CompilerParams(
            collective_id=0, has_side_effects=True, vmem_limit_bytes=32 << 20
        ),
    )(total, owner_map)


def solution(mesh):
    placed = (
        P(AXES, None, None),
        P(AXES, None),
        P(AXES, None, None),
        P(AXES, None),
        P(AXES),
        P(),
    )
    return jax.shard_map(
        shards,
        mesh=mesh,
        in_specs=placed,
        out_specs=P(AXES, None, None),
        check_vma=False,
    )
```

```python
import functools

import jax
import jax.numpy as jnp
from jax import lax
from jax.experimental import pallas as pl
from jax.experimental.pallas import tpu as pltpu
from jax.sharding import PartitionSpec as P

HR = 32
LW = 2
OWNMAX = 8
GROUP = 8
SPR = 8
AXES = ("wide", "narrow")


def kernel(a_hbm, cols, p_hbm, pattern, aggregate, g_ref,
           a_v, p_v, pooled, applied, rim, rim_side, a_sem, p_sem, send_sem, recv_sem):
    rows, nodes = a_hbm.shape[0], a_hbm.shape[1]
    me = lax.axis_index(AXES)
    groups = rows // GROUP
    shift = HR // GROUP
    narrow = lax.axis_size("narrow")
    count = lax.axis_size(AXES)
    mesh_id = pl.DeviceIdType.MESH
    others = [lax.rem(me + 1, count), lax.rem(me + count - 1, count)]
    others = [(other // narrow, lax.rem(other, narrow)) for other in others]
    barrier = pltpu.get_barrier_semaphore()
    for other in others:
        pl.semaphore_signal(barrier, inc=1, device_id=other, device_id_type=mesh_id)

    def p_copy(g):
        span = pl.ds(g * GROUP, GROUP)
        return pltpu.make_async_copy(p_hbm.at[span], p_v.at[span], p_sem.at[g])

    def a_copy(g):
        span = pl.ds(g * GROUP, GROUP)
        return pltpu.make_async_copy(a_hbm.at[span], a_v.at[span], a_sem.at[g])

    @pl.loop(0, groups)
    def _(step):
        p_copy(lax.rem(step + groups - shift, groups)).start()

    @pl.loop(0, groups)
    def _(g):
        a_copy(lax.rem(g + shift, groups)).start()

    left = lax.broadcasted_iota(jnp.int32, (nodes, 128), 1) < 64

    def place_group(step):
        g = lax.rem(step + groups - shift, groups)
        p_copy(g).wait()
        for j in range(GROUP):
            i = g * GROUP + j
            second = aggregate[i] - me * LW == 1
            has0 = pattern[i, 0] == 1
            has2 = pattern[i, 2] == 1
            x0 = p_v[i, :, :128]
            x2 = p_v[i, :, 128:]
            swapped = jnp.concatenate([x0[:, 64:], x0[:, :64]], axis=1)
            twice = jnp.concatenate([x2, x2], axis=1)
            bit = lambda flag: jnp.where(flag, 1.0, 0.0).astype(jnp.bfloat16)
            one = jnp.ones_like(x0)
            first_low = jnp.where(left, swapped, twice * bit(has2))
            second_low = x0 * jnp.where(left, one * bit(has0), one)
            pooled[HR + i, :, :128] = first_low * bit(~second) + second_low * bit(second)
            pooled[HR + i, :, 128:] = jnp.where(
                left, twice * bit(has2 & second), swapped * bit(has0 & ~second)
            )

    def rim_copies(side):
        spans = (
            (0, pl.ds(rows if side == 0 else HR, HR), pl.ds(0, 128), rim),
            (1, pl.ds(rows + HR - SPR if side == 0 else HR, SPR), pl.ds(128, 128), rim_side),
        )
        return [
            pltpu.make_async_remote_copy(
                src_ref=pooled.at[span, :, lanes],
                dst_ref=landing.at[side],
                send_sem=send_sem.at[side, half],
                recv_sem=recv_sem.at[side, half],
                device_id=others[side],
                device_id_type=mesh_id,
            )
            for half, span, lanes, landing in spans
        ]

    pl.loop(0, 2 * shift)(place_group)
    pl.semaphore_wait(barrier, 2)
    copies = rim_copies(0) + rim_copies(1)
    for copy in copies:
        copy.start()
    pl.loop(2 * shift, groups)(place_group)

    g_ref[...] = jnp.zeros_like(g_ref)
    base = HR - me * rows
    limit = pooled.shape[0] - 1

    def transposed_product(span_rows, lanes):
        left_rows = pooled[span_rows, :, lanes].reshape(GROUP * nodes, 128)
        return lax.dot_general(
            left_rows, applied[...], (((0,), (0,)), ((), ())), preferred_element_type=jnp.float32
        )

    def run_group(step):
        g = lax.rem(step + shift, groups)
        a_copy(g).wait()
        for j in range(GROUP):
            i = g * GROUP + j
            total = None
            for h in range(2):
                stack = jnp.concatenate(
                    [pooled[jnp.clip(cols[i, 4 * h + k] + base, 0, limit)] for k in range(4)], axis=0
                )
                part = jnp.dot(
                    a_v[i, :, 256 * h : 256 * (h + 1)], stack, preferred_element_type=jnp.float32
                )
                total = part if total is None else total + part
            applied[j * nodes : (j + 1) * nodes, :] = total.astype(jnp.bfloat16)
        g_ref[:128, :] += transposed_product(pl.ds(HR + g * GROUP, GROUP), pl.ds(0, 128))

        @pl.when((g == 0) | (g == groups - 1))
        def _():
            g_ref[128:, :] += transposed_product(pl.ds(HR + g * GROUP, GROUP), pl.ds(128, 128))

    inner = groups - 2 * shift
    pl.loop(0, inner)(run_group)
    for copy in copies:
        copy.wait()

    @pl.loop(0, HR)
    def _(i):
        for side, first in enumerate((0, rows + HR)):
            pooled[first + i, :, :128] = jnp.zeros((nodes, 128), jnp.bfloat16)
            pooled[first + i, :, 128:] = rim[side, i]

    @pl.loop(0, SPR)
    def _(i):
        for side, first in enumerate((HR - SPR, rows + HR)):
            pooled[first + i, :, :128] = rim_side[side, i]

    pl.loop(inner, groups)(run_group)


def gather_kernel(wide, narrow, total, owner_map, out, edge_out, edge_in, every,
                  edge_send, edge_recv, send_sem, recv_sem):
    w, n = lax.axis_index("wide"), lax.axis_index("narrow")
    me = w * narrow + n
    nodes = out.shape[1]
    count = wide * narrow
    following, preceding = lax.rem(me + 1, count), lax.rem(me + count - 1, count)
    beside = n + 1 - 2 * lax.rem(n, 2)
    across = lax.rem(n + 2, 4)
    mesh_id = pl.DeviceIdType.MESH

    barrier = pltpu.get_barrier_semaphore()
    for other in (following, preceding):
        pl.semaphore_signal(
            barrier, inc=1, device_id=(other // narrow, lax.rem(other, narrow)), device_id_type=mesh_id
        )
    for other in (beside, across):
        pl.semaphore_signal(barrier, inc=1, device_id=(w, other), device_id_type=mesh_id)

    def greet(d, carry):
        pl.semaphore_signal(
            barrier, inc=1, device_id=(lax.rem(w + d, wide), n), device_id_type=mesh_id
        )
        return carry

    lax.fori_loop(1, wide, greet, 0)

    edge_out[0] = total[2 * nodes : 3 * nodes, nodes : 3 * nodes]
    edge_out[1] = jnp.concatenate(
        [total[3 * nodes :, 3 * nodes :], total[3 * nodes :, :nodes]], axis=1
    )
    pl.semaphore_wait(barrier, wide + 3)

    def edge_copy(side, other):
        return pltpu.make_async_remote_copy(
            src_ref=edge_out.at[side],
            dst_ref=edge_in.at[side],
            send_sem=edge_send.at[side],
            recv_sem=edge_recv.at[side],
            device_id=(other // narrow, lax.rem(other, narrow)),
            device_id_type=mesh_id,
        )

    edges = [edge_copy(0, following), edge_copy(1, preceding)]
    for edge in edges:
        edge.start()
    for edge in edges:
        edge.wait()

    def store(slot, which, front, tail):
        every[slot, which, :64, :] = front.astype(jnp.bfloat16)
        tail = tail.astype(jnp.bfloat16)
        every[slot, which, 64:, :] = jnp.concatenate([tail[:32], tail[32:]], axis=1)

    own = jnp.concatenate([total[:nodes, 3 * nodes :], total[:nodes, :nodes]], axis=1)
    store(me, 0, own + edge_in[0], total[:nodes, nodes : 2 * nodes])
    own = total[nodes : 2 * nodes, : 2 * nodes]
    extra = edge_in[1]
    moved = jnp.concatenate([jnp.zeros_like(extra[:, :nodes]), extra[:, :nodes]], axis=1)
    last = total[nodes : 2 * nodes, 2 * nodes : 3 * nodes] + extra[:, nodes:]
    store(me, 1, own + moved, last)

    def copy(kind, d, slot, device):
        return pltpu.make_async_remote_copy(
            src_ref=every.at[slot],
            dst_ref=every.at[slot],
            send_sem=send_sem.at[kind, d],
            recv_sem=recv_sem.at[slot],
            device_id=device,
            device_id_type=mesh_id,
        )

    def along(d):
        return copy(0, d, me, (lax.rem(w + d, wide), n))

    def forward(d):
        slot = lax.rem(w + wide - d, wide) * narrow + n
        return copy(1, d, slot, (w, across)), copy(2, d, slot, (w, beside))

    def relay(d):
        slot = lax.rem(w + wide - d, wide) * narrow + across
        return copy(3, d, slot, (w, beside))

    def slot_at(d, column):
        return lax.rem(w + wide - d, wide) * narrow + column

    def send_along(d, carry):
        along(d).start()
        return carry

    lax.fori_loop(1, wide, send_along, 0)

    def pass_on(d, carry):
        @pl.when(d > 0)
        def _():
            copy(0, d, slot_at(d, n), (w, across)).wait_recv()

        for c in forward(d):
            c.start()
        return carry

    lax.fori_loop(0, wide, pass_on, 0)

    def pass_second(d, carry):
        copy(1, d, slot_at(d, across), (w, across)).wait_recv()
        relay(d).start()
        return carry

    lax.fori_loop(0, wide, pass_second, 0)

    def visit(a, found):
        hit = owner_map[a] == me
        rank = found[0]
        spots = tuple(
            jnp.where(hit & (rank == s), a, spot) for s, spot in enumerate(found[1:])
        )
        return (rank + jnp.where(hit, 1, 0),) + spots

    found = lax.fori_loop(
        0, owner_map.shape[0], visit, (jnp.int32(0),) + (jnp.int32(0),) * OWNMAX
    )

    across_beside = lax.rem(beside + 2, 4)

    def finish(d, carry):
        copy(2, d, slot_at(d, beside), (w, beside)).wait_recv()
        copy(3, d, slot_at(d, across_beside), (w, beside)).wait_recv()
        for c in forward(d):
            c.wait_send()
        relay(d).wait_send()

        @pl.when(d > 0)
        def _():
            along(d).wait_send()

        return carry

    lax.fori_loop(0, wide, finish, 0)

    for s in range(OWNMAX):
        spot = found[1 + s]
        keep = jnp.where(s < found[0], 1.0, 0.0)
        row = every[spot // LW, lax.rem(spot, LW)].astype(jnp.float32) * keep
        row = row.astype(jnp.bfloat16)
        out[s, :, :128] = row[:64]
        out[s, :32, 128:] = row[64:, :64]
        out[s, 32:, 128:] = row[64:, 64:]


def shards(a_blocks, a_columns, p_blocks, p_pattern, aggregate, owner_map):
    rows, nodes = a_blocks.shape[:2]
    count = lax.axis_size(AXES)
    vmem = pl.BlockSpec(memory_space=pltpu.VMEM)
    smem = pl.BlockSpec(memory_space=pltpu.SMEM)
    hbm = pl.BlockSpec(memory_space=pl.ANY)
    groups = rows // GROUP
    total = pl.pallas_call(
        kernel,
        out_shape=jax.ShapeDtypeStruct((4 * nodes, 4 * nodes), jnp.float32),
        in_specs=[hbm, smem, hbm, smem, smem],
        out_specs=vmem,
        scratch_shapes=[
            pltpu.VMEM(a_blocks.shape, jnp.bfloat16),
            pltpu.VMEM(p_blocks.shape, jnp.bfloat16),
            pltpu.VMEM((rows + 2 * HR, nodes, 4 * nodes), jnp.bfloat16),
            pltpu.VMEM((GROUP * nodes, 4 * nodes), jnp.bfloat16),
            pltpu.VMEM((2, HR, nodes, 2 * nodes), jnp.bfloat16),
            pltpu.VMEM((2, SPR, nodes, 2 * nodes), jnp.bfloat16),
            pltpu.SemaphoreType.DMA((groups,)),
            pltpu.SemaphoreType.DMA((groups,)),
            pltpu.SemaphoreType.DMA((2, 2)),
            pltpu.SemaphoreType.DMA((2, 2)),
        ],
        compiler_params=pltpu.CompilerParams(
            collective_id=1, has_side_effects=True, vmem_limit_bytes=48 << 20
        ),
    )(a_blocks, a_columns, p_blocks, p_pattern, aggregate)
    wide, narrow = lax.axis_size("wide"), lax.axis_size("narrow")
    return pl.pallas_call(
        functools.partial(gather_kernel, wide, narrow),
        out_shape=jax.ShapeDtypeStruct((OWNMAX, nodes, 3 * nodes), jnp.bfloat16),
        in_specs=[vmem, smem],
        out_specs=vmem,
        scratch_shapes=[
            pltpu.VMEM((2, nodes, 2 * nodes), jnp.float32),
            pltpu.VMEM((2, nodes, 2 * nodes), jnp.float32),
            pltpu.VMEM((count, LW, 96, 128), jnp.bfloat16),
            pltpu.SemaphoreType.DMA((2,)),
            pltpu.SemaphoreType.DMA((2,)),
            pltpu.SemaphoreType.DMA((4, wide)),
            pltpu.SemaphoreType.DMA((count,)),
        ],
        compiler_params=pltpu.CompilerParams(
            collective_id=0, has_side_effects=True, vmem_limit_bytes=32 << 20
        ),
    )(total, owner_map)


def solution(mesh):
    placed = (
        P(AXES, None, None),
        P(AXES, None),
        P(AXES, None, None),
        P(AXES, None),
        P(AXES),
        P(),
    )
    return jax.shard_map(
        shards,
        mesh=mesh,
        in_specs=placed,
        out_specs=P(AXES, None, None),
        check_vma=False,
    )
```

```python
import functools

import jax
import jax.numpy as jnp
from jax import lax
from jax.experimental import pallas as pl
from jax.experimental.pallas import tpu as pltpu
from jax.sharding import PartitionSpec as P

HR = 32
LW = 2
OWNMAX = 8
GROUP = 8
SPR = 8
AXES = ("wide", "narrow")


def kernel(a_hbm, cols, p_hbm, pattern, aggregate, g_ref,
           a_v, p_v, pooled, applied, rim, rim_side, a_sem, p_sem, send_sem, recv_sem):
    rows, nodes = a_hbm.shape[0], a_hbm.shape[1]
    me = lax.axis_index(AXES)
    groups = rows // GROUP
    shift = HR // GROUP
    first_inner = (HR + SPR) // GROUP
    narrow = lax.axis_size("narrow")
    count = lax.axis_size(AXES)
    mesh_id = pl.DeviceIdType.MESH
    others = [lax.rem(me + 1, count), lax.rem(me + count - 1, count)]
    others = [(other // narrow, lax.rem(other, narrow)) for other in others]
    barrier = pltpu.get_barrier_semaphore()
    for other in others:
        pl.semaphore_signal(barrier, inc=1, device_id=other, device_id_type=mesh_id)

    def p_copy(g):
        span = pl.ds(g * GROUP, GROUP)
        return pltpu.make_async_copy(p_hbm.at[span], p_v.at[span], p_sem.at[g])

    def a_copy(g):
        span = pl.ds(g * GROUP, GROUP)
        return pltpu.make_async_copy(a_hbm.at[span], a_v.at[span], a_sem.at[g])

    @pl.loop(0, groups)
    def _(step):
        p_copy(lax.rem(step + groups - shift, groups)).start()

    @pl.loop(0, groups)
    def _(g):
        a_copy(lax.rem(g + first_inner, groups)).start()

    left = lax.broadcasted_iota(jnp.int32, (nodes, 128), 1) < 64

    def place_group(step, at_end):
        g = lax.rem(step + groups - shift, groups)
        p_copy(g).wait()
        for j in range(GROUP):
            i = g * GROUP + j
            second = aggregate[i] - me * LW == 1
            has0 = pattern[i, 0] == 1
            has2 = pattern[i, 2] == 1
            x0 = p_v[i, :, :128]
            x2 = p_v[i, :, 128:]
            swapped = jnp.concatenate([x0[:, 64:], x0[:, :64]], axis=1)
            twice = jnp.concatenate([x2, x2], axis=1)
            bit = lambda flag: jnp.where(flag, 1.0, 0.0).astype(jnp.bfloat16)
            one = jnp.ones_like(x0)
            first_low = jnp.where(left, swapped, twice * bit(has2))
            second_low = x0 * jnp.where(left, one * bit(has0), one)
            pooled[HR + i, :, :128] = first_low * bit(~second) + second_low * bit(second)
            if at_end:
                pooled[HR + i, :, 128:] = jnp.where(
                    left, twice * bit(has2 & second), swapped * bit(has0 & ~second)
                )
            else:
                pooled[HR + i, :, 128:] = jnp.zeros_like(x0)

    def rim_copies(side):
        spans = (
            (0, pl.ds(rows if side == 0 else HR, HR), pl.ds(0, 128), rim),
            (1, pl.ds(rows + HR - SPR if side == 0 else HR, SPR), pl.ds(128, 128), rim_side),
        )
        return [
            pltpu.make_async_remote_copy(
                src_ref=pooled.at[span, :, lanes],
                dst_ref=landing.at[side],
                send_sem=send_sem.at[side, half],
                recv_sem=recv_sem.at[side, half],
                device_id=others[side],
                device_id_type=mesh_id,
            )
            for half, span, lanes, landing in spans
        ]

    pl.loop(0, 2 * shift)(functools.partial(place_group, at_end=True))
    pl.semaphore_wait(barrier, 2)
    copies = rim_copies(0) + rim_copies(1)
    for copy in copies:
        copy.start()
    pl.loop(2 * shift, groups)(functools.partial(place_group, at_end=False))

    g_ref[...] = jnp.zeros_like(g_ref)
    base = HR - me * rows
    limit = pooled.shape[0] - 1

    def transposed_product(span_rows, lanes, width):
        left_rows = pooled[span_rows, :, lanes].reshape(GROUP * nodes, 128)
        return lax.dot_general(
            left_rows, applied[:, :width], (((0,), (0,)), ((), ())), preferred_element_type=jnp.float32
        )

    def run_group(step, width):
        g = lax.rem(step + first_inner, groups)
        a_copy(g).wait()
        for j in range(GROUP):
            i = g * GROUP + j
            total = None
            for h in range(2):
                stack = jnp.concatenate(
                    [
                        pooled[jnp.clip(cols[i, 4 * h + k] + base, 0, limit), :, :width]
                        for k in range(4)
                    ],
                    axis=0,
                )
                part = jnp.dot(
                    a_v[i, :, 256 * h : 256 * (h + 1)], stack, preferred_element_type=jnp.float32
                )
                total = part if total is None else total + part
            applied[j * nodes : (j + 1) * nodes, :width] = total.astype(jnp.bfloat16)
        span = pl.ds(HR + g * GROUP, GROUP)
        g_ref[:128, :width] += transposed_product(span, pl.ds(0, 128), width)
        if width == 128:
            return

        @pl.when((g == 0) | (g == groups - 1))
        def _():
            g_ref[128:, :] += transposed_product(span, pl.ds(128, 128), width)

    inner = groups - 2 * first_inner
    pl.loop(0, inner)(functools.partial(run_group, width=128))
    for copy in copies:
        copy.wait()

    @pl.loop(0, HR)
    def _(i):
        for side, first in enumerate((0, rows + HR)):
            pooled[first + i, :, :128] = jnp.zeros((nodes, 128), jnp.bfloat16)
            pooled[first + i, :, 128:] = rim[side, i]

    @pl.loop(0, SPR)
    def _(i):
        for side, first in enumerate((HR - SPR, rows + HR)):
            pooled[first + i, :, :128] = rim_side[side, i]

    pl.loop(inner, groups)(functools.partial(run_group, width=256))


def gather_kernel(wide, narrow, total, owner_map, out, edge_out, edge_in, every,
                  edge_send, edge_recv, send_sem, recv_sem):
    w, n = lax.axis_index("wide"), lax.axis_index("narrow")
    me = w * narrow + n
    nodes = out.shape[1]
    count = wide * narrow
    following, preceding = lax.rem(me + 1, count), lax.rem(me + count - 1, count)
    beside = n + 1 - 2 * lax.rem(n, 2)
    across = lax.rem(n + 2, 4)
    mesh_id = pl.DeviceIdType.MESH

    barrier = pltpu.get_barrier_semaphore()
    for other in (following, preceding):
        pl.semaphore_signal(
            barrier, inc=1, device_id=(other // narrow, lax.rem(other, narrow)), device_id_type=mesh_id
        )
    for other in (beside, across):
        pl.semaphore_signal(barrier, inc=1, device_id=(w, other), device_id_type=mesh_id)

    def greet(d, carry):
        pl.semaphore_signal(
            barrier, inc=1, device_id=(lax.rem(w + d, wide), n), device_id_type=mesh_id
        )
        return carry

    lax.fori_loop(1, wide, greet, 0)

    edge_out[0] = total[2 * nodes : 3 * nodes, nodes : 3 * nodes]
    edge_out[1] = jnp.concatenate(
        [total[3 * nodes :, 3 * nodes :], total[3 * nodes :, :nodes]], axis=1
    )
    pl.semaphore_wait(barrier, wide + 3)

    def edge_copy(side, other):
        return pltpu.make_async_remote_copy(
            src_ref=edge_out.at[side],
            dst_ref=edge_in.at[side],
            send_sem=edge_send.at[side],
            recv_sem=edge_recv.at[side],
            device_id=(other // narrow, lax.rem(other, narrow)),
            device_id_type=mesh_id,
        )

    edges = [edge_copy(0, following), edge_copy(1, preceding)]
    for edge in edges:
        edge.start()
    def visit(a, found):
        hit = owner_map[a] == me
        rank = found[0]
        spots = tuple(
            jnp.where(hit & (rank == s), a, spot) for s, spot in enumerate(found[1:])
        )
        return (rank + jnp.where(hit, 1, 0),) + spots

    found = lax.fori_loop(
        0, owner_map.shape[0], visit, (jnp.int32(0),) + (jnp.int32(0),) * OWNMAX
    )

    for edge in edges:
        edge.wait()

    def store(slot, which, front, tail):
        every[slot, which, :64, :] = front.astype(jnp.bfloat16)
        tail = tail.astype(jnp.bfloat16)
        every[slot, which, 64:, :] = jnp.concatenate([tail[:32], tail[32:]], axis=1)

    own = jnp.concatenate([total[:nodes, 3 * nodes :], total[:nodes, :nodes]], axis=1)
    store(me, 0, own + edge_in[0], total[:nodes, nodes : 2 * nodes])
    own = total[nodes : 2 * nodes, : 2 * nodes]
    extra = edge_in[1]
    moved = jnp.concatenate([jnp.zeros_like(extra[:, :nodes]), extra[:, :nodes]], axis=1)
    last = total[nodes : 2 * nodes, 2 * nodes : 3 * nodes] + extra[:, nodes:]
    store(me, 1, own + moved, last)

    def copy(kind, d, slot, device):
        return pltpu.make_async_remote_copy(
            src_ref=every.at[slot],
            dst_ref=every.at[slot],
            send_sem=send_sem.at[kind, d],
            recv_sem=recv_sem.at[slot],
            device_id=device,
            device_id_type=mesh_id,
        )

    def along(d):
        return copy(0, d, me, (lax.rem(w + d, wide), n))

    def forward(d):
        slot = lax.rem(w + wide - d, wide) * narrow + n
        return copy(1, d, slot, (w, across)), copy(2, d, slot, (w, beside))

    def relay(d):
        slot = lax.rem(w + wide - d, wide) * narrow + across
        return copy(3, d, slot, (w, beside))

    def slot_at(d, column):
        return lax.rem(w + wide - d, wide) * narrow + column

    def send_along(d, carry):
        along(d).start()
        return carry

    lax.fori_loop(1, wide, send_along, 0)

    def pass_on(d, carry):
        @pl.when(d > 0)
        def _():
            copy(0, d, slot_at(d, n), (w, across)).wait_recv()

        for c in forward(d):
            c.start()
        return carry

    lax.fori_loop(0, wide, pass_on, 0)

    def pass_second(d, carry):
        copy(1, d, slot_at(d, across), (w, across)).wait_recv()
        relay(d).start()
        return carry

    lax.fori_loop(0, wide, pass_second, 0)

    across_beside = lax.rem(beside + 2, 4)

    def finish(d, carry):
        copy(2, d, slot_at(d, beside), (w, beside)).wait_recv()
        copy(3, d, slot_at(d, across_beside), (w, beside)).wait_recv()
        for c in forward(d):
            c.wait_send()
        relay(d).wait_send()

        @pl.when(d > 0)
        def _():
            along(d).wait_send()

        return carry

    lax.fori_loop(0, wide, finish, 0)

    for s in range(OWNMAX):
        spot = found[1 + s]
        keep = jnp.where(s < found[0], 1.0, 0.0)
        row = every[spot // LW, lax.rem(spot, LW)].astype(jnp.float32) * keep
        row = row.astype(jnp.bfloat16)
        out[s, :, :128] = row[:64]
        out[s, :32, 128:] = row[64:, :64]
        out[s, 32:, 128:] = row[64:, 64:]


def shards(a_blocks, a_columns, p_blocks, p_pattern, aggregate, owner_map):
    rows, nodes = a_blocks.shape[:2]
    count = lax.axis_size(AXES)
    vmem = pl.BlockSpec(memory_space=pltpu.VMEM)
    smem = pl.BlockSpec(memory_space=pltpu.SMEM)
    hbm = pl.BlockSpec(memory_space=pl.ANY)
    groups = rows // GROUP
    total = pl.pallas_call(
        kernel,
        out_shape=jax.ShapeDtypeStruct((4 * nodes, 4 * nodes), jnp.float32),
        in_specs=[hbm, smem, hbm, smem, smem],
        out_specs=vmem,
        scratch_shapes=[
            pltpu.VMEM(a_blocks.shape, jnp.bfloat16),
            pltpu.VMEM(p_blocks.shape, jnp.bfloat16),
            pltpu.VMEM((rows + 2 * HR, nodes, 4 * nodes), jnp.bfloat16),
            pltpu.VMEM((GROUP * nodes, 4 * nodes), jnp.bfloat16),
            pltpu.VMEM((2, HR, nodes, 2 * nodes), jnp.bfloat16),
            pltpu.VMEM((2, SPR, nodes, 2 * nodes), jnp.bfloat16),
            pltpu.SemaphoreType.DMA((groups,)),
            pltpu.SemaphoreType.DMA((groups,)),
            pltpu.SemaphoreType.DMA((2, 2)),
            pltpu.SemaphoreType.DMA((2, 2)),
        ],
        compiler_params=pltpu.CompilerParams(
            collective_id=1, has_side_effects=True, vmem_limit_bytes=48 << 20
        ),
    )(a_blocks, a_columns, p_blocks, p_pattern, aggregate)
    wide, narrow = lax.axis_size("wide"), lax.axis_size("narrow")
    return pl.pallas_call(
        functools.partial(gather_kernel, wide, narrow),
        out_shape=jax.ShapeDtypeStruct((OWNMAX, nodes, 3 * nodes), jnp.bfloat16),
        in_specs=[vmem, smem],
        out_specs=vmem,
        scratch_shapes=[
            pltpu.VMEM((2, nodes, 2 * nodes), jnp.float32),
            pltpu.VMEM((2, nodes, 2 * nodes), jnp.float32),
            pltpu.VMEM((count, LW, 96, 128), jnp.bfloat16),
            pltpu.SemaphoreType.DMA((2,)),
            pltpu.SemaphoreType.DMA((2,)),
            pltpu.SemaphoreType.DMA((4, wide)),
            pltpu.SemaphoreType.DMA((count,)),
        ],
        compiler_params=pltpu.CompilerParams(
            collective_id=0, has_side_effects=True, vmem_limit_bytes=32 << 20
        ),
    )(total, owner_map)


def solution(mesh):
    placed = (
        P(AXES, None, None),
        P(AXES, None),
        P(AXES, None, None),
        P(AXES, None),
        P(AXES),
        P(),
    )
    return jax.shard_map(
        shards,
        mesh=mesh,
        in_specs=placed,
        out_specs=P(AXES, None, None),
        check_vma=False,
    )
```

```python
import functools

import jax
import jax.numpy as jnp
from jax import lax
from jax.experimental import pallas as pl
from jax.experimental.pallas import tpu as pltpu
from jax.sharding import PartitionSpec as P

HR = 32
LW = 2
OWNMAX = 8
GROUP = 8
SPR = 8
AXES = ("wide", "narrow")


def kernel(a_hbm, cols, p_hbm, pattern, aggregate, g_ref,
           a_v, p_v, pooled, applied, packed, rim, rim_side, a_sem, p_sem, send_sem, recv_sem):
    rows, nodes = a_hbm.shape[0], a_hbm.shape[1]
    me = lax.axis_index(AXES)
    groups = rows // GROUP
    shift = HR // GROUP
    first_inner = (HR + SPR) // GROUP
    narrow = lax.axis_size("narrow")
    count = lax.axis_size(AXES)
    mesh_id = pl.DeviceIdType.MESH
    others = [lax.rem(me + 1, count), lax.rem(me + count - 1, count)]
    others = [(other // narrow, lax.rem(other, narrow)) for other in others]
    barrier = pltpu.get_barrier_semaphore()
    for other in others:
        pl.semaphore_signal(barrier, inc=1, device_id=other, device_id_type=mesh_id)

    def p_copy(g):
        span = pl.ds(g * GROUP, GROUP)
        return pltpu.make_async_copy(p_hbm.at[span], p_v.at[span], p_sem.at[g])

    def a_copy(g):
        span = pl.ds(g * GROUP, GROUP)
        return pltpu.make_async_copy(a_hbm.at[span], a_v.at[span], a_sem.at[g])

    @pl.loop(0, groups)
    def _(step):
        p_copy(lax.rem(step + groups - shift, groups)).start()

    @pl.loop(0, groups)
    def _(g):
        a_copy(lax.rem(g + first_inner, groups)).start()

    left = lax.broadcasted_iota(jnp.int32, (nodes, 128), 1) < 64

    def place_group(step, at_end):
        g = lax.rem(step + groups - shift, groups)
        p_copy(g).wait()
        for j in range(GROUP):
            i = g * GROUP + j
            second = aggregate[i] - me * LW == 1
            has0 = pattern[i, 0] == 1
            has2 = pattern[i, 2] == 1
            x0 = p_v[i, :, :128]
            x2 = p_v[i, :, 128:]
            swapped = jnp.concatenate([x0[:, 64:], x0[:, :64]], axis=1)
            twice = jnp.concatenate([x2, x2], axis=1)
            bit = lambda flag: jnp.where(flag, 1.0, 0.0).astype(jnp.bfloat16)
            one = jnp.ones_like(x0)
            first_low = jnp.where(left, swapped, twice * bit(has2))
            second_low = x0 * jnp.where(left, one * bit(has0), one)
            pooled[HR + i, :, :128] = first_low * bit(~second) + second_low * bit(second)
            if at_end:
                pooled[HR + i, :, 128:] = jnp.where(
                    left, twice * bit(has2 & second), swapped * bit(has0 & ~second)
                )
            else:
                pooled[HR + i, :, 128:] = jnp.zeros_like(x0)

    def rim_copies(side):
        end = pl.ds(rows + HR - SPR if side == 0 else HR, SPR)
        pairs = (
            (packed.at[side], rim.at[side]),
            (pooled.at[end, :, pl.ds(128, 128)], rim_side.at[side]),
        )
        return [
            pltpu.make_async_remote_copy(
                src_ref=source,
                dst_ref=landing,
                send_sem=send_sem.at[side, half],
                recv_sem=recv_sem.at[side, half],
                device_id=others[side],
                device_id_type=mesh_id,
            )
            for half, (source, landing) in enumerate(pairs)
        ]

    pl.loop(0, 2 * shift)(functools.partial(place_group, at_end=True))

    @pl.loop(0, HR // 2)
    def _(i):
        for side, first, at in ((0, rows, 64), (1, HR, 0)):
            packed[side, i] = jnp.concatenate(
                [pooled[first + i + k, :, at : at + 64] for k in (0, HR // 2)], axis=1
            )

    pl.semaphore_wait(barrier, 2)
    copies = rim_copies(0) + rim_copies(1)
    for copy in copies:
        copy.start()
    pl.loop(2 * shift, groups)(functools.partial(place_group, at_end=False))

    g_ref[...] = jnp.zeros_like(g_ref)
    base = HR - me * rows
    limit = pooled.shape[0] - 1

    def transposed_product(span_rows, lanes, width):
        left_rows = pooled[span_rows, :, lanes].reshape(GROUP * nodes, 128)
        return lax.dot_general(
            left_rows, applied[:, :width], (((0,), (0,)), ((), ())), preferred_element_type=jnp.float32
        )

    def run_group(step, width):
        g = lax.rem(step + first_inner, groups)
        a_copy(g).wait()
        for j in range(GROUP):
            i = g * GROUP + j
            total = None
            for h in range(2):
                stack = jnp.concatenate(
                    [
                        pooled[jnp.clip(cols[i, 4 * h + k] + base, 0, limit), :, :width]
                        for k in range(4)
                    ],
                    axis=0,
                )
                part = jnp.dot(
                    a_v[i, :, 256 * h : 256 * (h + 1)], stack, preferred_element_type=jnp.float32
                )
                total = part if total is None else total + part
            applied[j * nodes : (j + 1) * nodes, :width] = total.astype(jnp.bfloat16)
        span = pl.ds(HR + g * GROUP, GROUP)
        g_ref[:128, :width] += transposed_product(span, pl.ds(0, 128), width)
        if width == 128:
            return

        @pl.when((g == 0) | (g == groups - 1))
        def _():
            g_ref[128:, :] += transposed_product(span, pl.ds(128, 128), width)

    inner = groups - 2 * first_inner
    pl.loop(0, inner)(functools.partial(run_group, width=128))
    for copy in copies:
        copy.wait()

    @pl.loop(0, HR // 2)
    def _(i):
        blank = jnp.zeros((nodes, 64), jnp.bfloat16)
        for side, first in enumerate((0, rows + HR)):
            for k in range(2):
                row = first + i + k * (HR // 2)
                own = rim[side, i, :, 64 * k : 64 * (k + 1)]
                pooled[row, :, :128] = jnp.zeros((nodes, 128), jnp.bfloat16)
                pooled[row, :, 128:] = jnp.concatenate(
                    [blank, own] if side == 0 else [own, blank], axis=1
                )

    @pl.loop(0, SPR)
    def _(i):
        for side, first in enumerate((HR - SPR, rows + HR)):
            pooled[first + i, :, :128] = rim_side[side, i]

    pl.loop(inner, groups)(functools.partial(run_group, width=256))


def gather_kernel(wide, narrow, total, owner_map, out, edge_out, edge_in, every,
                  edge_send, edge_recv, send_sem, recv_sem):
    w, n = lax.axis_index("wide"), lax.axis_index("narrow")
    me = w * narrow + n
    nodes = out.shape[1]
    count = wide * narrow
    following, preceding = lax.rem(me + 1, count), lax.rem(me + count - 1, count)
    beside = n + 1 - 2 * lax.rem(n, 2)
    across = lax.rem(n + 2, 4)
    mesh_id = pl.DeviceIdType.MESH

    barrier = pltpu.get_barrier_semaphore()
    for other in (following, preceding):
        pl.semaphore_signal(
            barrier, inc=1, device_id=(other // narrow, lax.rem(other, narrow)), device_id_type=mesh_id
        )
    for other in (beside, across):
        pl.semaphore_signal(barrier, inc=1, device_id=(w, other), device_id_type=mesh_id)

    def greet(d, carry):
        pl.semaphore_signal(
            barrier, inc=1, device_id=(lax.rem(w + d, wide), n), device_id_type=mesh_id
        )
        return carry

    lax.fori_loop(1, wide, greet, 0)

    edge_out[0] = total[2 * nodes : 3 * nodes, nodes : 3 * nodes]
    edge_out[1] = jnp.concatenate(
        [total[3 * nodes :, 3 * nodes :], total[3 * nodes :, :nodes]], axis=1
    )
    pl.semaphore_wait(barrier, wide + 3)

    def edge_copy(side, other):
        return pltpu.make_async_remote_copy(
            src_ref=edge_out.at[side],
            dst_ref=edge_in.at[side],
            send_sem=edge_send.at[side],
            recv_sem=edge_recv.at[side],
            device_id=(other // narrow, lax.rem(other, narrow)),
            device_id_type=mesh_id,
        )

    edges = [edge_copy(0, following), edge_copy(1, preceding)]
    for edge in edges:
        edge.start()
    def visit(a, found):
        hit = owner_map[a] == me
        rank = found[0]
        spots = tuple(
            jnp.where(hit & (rank == s), a, spot) for s, spot in enumerate(found[1:])
        )
        return (rank + jnp.where(hit, 1, 0),) + spots

    found = lax.fori_loop(
        0, owner_map.shape[0], visit, (jnp.int32(0),) + (jnp.int32(0),) * OWNMAX
    )

    for edge in edges:
        edge.wait()

    def store(slot, which, front, tail):
        every[slot, which, :64, :] = front.astype(jnp.bfloat16)
        tail = tail.astype(jnp.bfloat16)
        every[slot, which, 64:, :] = jnp.concatenate([tail[:32], tail[32:]], axis=1)

    own = jnp.concatenate([total[:nodes, 3 * nodes :], total[:nodes, :nodes]], axis=1)
    store(me, 0, own + edge_in[0], total[:nodes, nodes : 2 * nodes])
    own = total[nodes : 2 * nodes, : 2 * nodes]
    extra = edge_in[1]
    moved = jnp.concatenate([jnp.zeros_like(extra[:, :nodes]), extra[:, :nodes]], axis=1)
    last = total[nodes : 2 * nodes, 2 * nodes : 3 * nodes] + extra[:, nodes:]
    store(me, 1, own + moved, last)

    def copy(kind, d, slot, device):
        return pltpu.make_async_remote_copy(
            src_ref=every.at[slot],
            dst_ref=every.at[slot],
            send_sem=send_sem.at[kind, d],
            recv_sem=recv_sem.at[slot],
            device_id=device,
            device_id_type=mesh_id,
        )

    def along(d):
        return copy(0, d, me, (lax.rem(w + d, wide), n))

    def forward(d):
        slot = lax.rem(w + wide - d, wide) * narrow + n
        return copy(1, d, slot, (w, across)), copy(2, d, slot, (w, beside))

    def relay(d):
        slot = lax.rem(w + wide - d, wide) * narrow + across
        return copy(3, d, slot, (w, beside))

    def slot_at(d, column):
        return lax.rem(w + wide - d, wide) * narrow + column

    def send_along(d, carry):
        along(d).start()
        return carry

    lax.fori_loop(1, wide, send_along, 0)

    def pass_on(d, carry):
        @pl.when(d > 0)
        def _():
            copy(0, d, slot_at(d, n), (w, across)).wait_recv()

        for c in forward(d):
            c.start()
        return carry

    lax.fori_loop(0, wide, pass_on, 0)

    def pass_second(d, carry):
        copy(1, d, slot_at(d, across), (w, across)).wait_recv()
        relay(d).start()
        return carry

    lax.fori_loop(0, wide, pass_second, 0)

    across_beside = lax.rem(beside + 2, 4)

    def finish(d, carry):
        copy(2, d, slot_at(d, beside), (w, beside)).wait_recv()
        copy(3, d, slot_at(d, across_beside), (w, beside)).wait_recv()
        for c in forward(d):
            c.wait_send()
        relay(d).wait_send()

        @pl.when(d > 0)
        def _():
            along(d).wait_send()

        return carry

    lax.fori_loop(0, wide, finish, 0)

    for s in range(OWNMAX):
        spot = found[1 + s]
        keep = jnp.where(s < found[0], 1.0, 0.0)
        row = every[spot // LW, lax.rem(spot, LW)].astype(jnp.float32) * keep
        row = row.astype(jnp.bfloat16)
        out[s, :, :128] = row[:64]
        out[s, :32, 128:] = row[64:, :64]
        out[s, 32:, 128:] = row[64:, 64:]


def shards(a_blocks, a_columns, p_blocks, p_pattern, aggregate, owner_map):
    rows, nodes = a_blocks.shape[:2]
    count = lax.axis_size(AXES)
    vmem = pl.BlockSpec(memory_space=pltpu.VMEM)
    smem = pl.BlockSpec(memory_space=pltpu.SMEM)
    hbm = pl.BlockSpec(memory_space=pl.ANY)
    groups = rows // GROUP
    total = pl.pallas_call(
        kernel,
        out_shape=jax.ShapeDtypeStruct((4 * nodes, 4 * nodes), jnp.float32),
        in_specs=[hbm, smem, hbm, smem, smem],
        out_specs=vmem,
        scratch_shapes=[
            pltpu.VMEM(a_blocks.shape, jnp.bfloat16),
            pltpu.VMEM(p_blocks.shape, jnp.bfloat16),
            pltpu.VMEM((rows + 2 * HR, nodes, 4 * nodes), jnp.bfloat16),
            pltpu.VMEM((GROUP * nodes, 4 * nodes), jnp.bfloat16),
            pltpu.VMEM((2, HR // 2, nodes, 2 * nodes), jnp.bfloat16),
            pltpu.VMEM((2, HR // 2, nodes, 2 * nodes), jnp.bfloat16),
            pltpu.VMEM((2, SPR, nodes, 2 * nodes), jnp.bfloat16),
            pltpu.SemaphoreType.DMA((groups,)),
            pltpu.SemaphoreType.DMA((groups,)),
            pltpu.SemaphoreType.DMA((2, 2)),
            pltpu.SemaphoreType.DMA((2, 2)),
        ],
        compiler_params=pltpu.CompilerParams(
            collective_id=1, has_side_effects=True, vmem_limit_bytes=48 << 20
        ),
    )(a_blocks, a_columns, p_blocks, p_pattern, aggregate)
    wide, narrow = lax.axis_size("wide"), lax.axis_size("narrow")
    return pl.pallas_call(
        functools.partial(gather_kernel, wide, narrow),
        out_shape=jax.ShapeDtypeStruct((OWNMAX, nodes, 3 * nodes), jnp.bfloat16),
        in_specs=[vmem, smem],
        out_specs=vmem,
        scratch_shapes=[
            pltpu.VMEM((2, nodes, 2 * nodes), jnp.float32),
            pltpu.VMEM((2, nodes, 2 * nodes), jnp.float32),
            pltpu.VMEM((count, LW, 96, 128), jnp.bfloat16),
            pltpu.SemaphoreType.DMA((2,)),
            pltpu.SemaphoreType.DMA((2,)),
            pltpu.SemaphoreType.DMA((4, wide)),
            pltpu.SemaphoreType.DMA((count,)),
        ],
        compiler_params=pltpu.CompilerParams(
            collective_id=0, has_side_effects=True, vmem_limit_bytes=32 << 20
        ),
    )(total, owner_map)


def solution(mesh):
    placed = (
        P(AXES, None, None),
        P(AXES, None),
        P(AXES, None, None),
        P(AXES, None),
        P(AXES),
        P(),
    )
    return jax.shard_map(
        shards,
        mesh=mesh,
        in_specs=placed,
        out_specs=P(AXES, None, None),
        check_vma=False,
    )
```
